32 devices in a mesh: grp: 2 (over x), ctx: 16 (over z, y, core).
Axes of the slice: x: 2, y: 2, z: 4, core: 2. Of those that a mesh axis runs over, the one named last changes fastest.
Arguments:
- query: bfloat16 [16384, 2048], P(('grp', 'ctx')), parts along dimension 0, may hold values from -6 to 6
- key: bfloat16 [16384, 2048], P(('grp', 'ctx')), parts along dimension 0, may hold values from -6 to 6
- value: bfloat16 [16384, 2048], P(('grp', 'ctx')), parts along dimension 0, may hold values from -6 to 6
- doc_ids: int32 [16384], P(('grp', 'ctx')), parts along dimension 0, may hold values from 0 to 7, never falling along the last dimension, each value on 1 to 4096 neighbouring positions
- gates: bfloat16 [16384, 256], P(('grp', 'ctx')), parts along dimension 0, may hold values from 0.049804688 to 1
- gain: float32 [2048], replicated, may hold values from 0.5 to 1.5
Outputs:
- mixed: bfloat16 [16384, 2048], P(('grp', 'ctx')), parts along dimension 0
The draws below stay inside these ranges and needn't reach their ends.
There are 2 independent parts, one for each index of `grp`. The reference program is written for one: setup_inputs(seed, part) draws one part's arguments, and reference() takes and returns one part's arrays. A program takes and returns all parts, laid end to end along the dimension named above; an argument that names none is the same for every part. Nothing has to cross between parts.
Inputs may be any that keep to these rules, and one draw needn't show every extreme that they name: `doc_ids`: document ids never fall along the window, every id from 0 to 7 occurs, and one document covers 8192 // 2 positions.
All inputs are finite; a program needn't handle non-finite values.
Results may differ from the reference program's by a relative error of at most 0.0045.
Values may be sent and summed in bfloat16 or wider, within the bound.
A program may use at most 128 MiB of HBM per device.

```python
import math
import jax
import jax.numpy as jnp
import numpy as np
from jax import lax

H = 16
DK = 128
LEVELS = 16
TOK_DEV = 512
DOCS = 8
TOKENS = 8192
LOGCTX = 4
N_CTX = 16


def block_scale(key, dims, split, smallest, high):
    loudness, own = 1.0, jax.random.fold_in(key, 6)
    for axis_at, blocks in split:
        heights = jnp.exp(jax.random.uniform(jax.random.fold_in(own, axis_at), (blocks,), jnp.float32, smallest / len(split), high / len(split)))
        loudness = loudness * jnp.repeat(heights, dims[axis_at] // blocks).reshape([-1 if axis == axis_at else 1 for axis in range(len(dims))])
    return loudness


def length_profile(number_of, total, reach, slope):
    loads = [(1 << 20) // math.isqrt(grade ** slope) + 1 for grade in range(2, number_of + 1)]
    rest, holding = total - reach - (number_of - 1), [1] * (number_of - 1)
    while rest > 0:
        movable = [i for i in range(number_of - 1) if holding[i] < reach]
        pool, remaining = sum([loads[i] for i in movable]), rest
        for i in movable:
            more = min(reach - holding[i], max(1, remaining * loads[i] // pool), rest)
            holding[i] = holding[i] + more
            rest = rest - more
    return np.array([reach] + holding)


def uneven_parts(key, count, total, limit, lean):
    if count == 2:
        one = jax.random.randint(key, (), max(1, total - limit), min(limit, total - 1) + 1)
        return jnp.stack([one, total - one])
    lengths = jnp.asarray(length_profile(count, total, limit, lean), jnp.int32)
    couples = (count - 1) // 2
    giver, taker = lengths[1:1 + 2 * couples:2], lengths[2:2 + 2 * couples:2]
    room = jnp.minimum(giver - 1, limit - taker)
    passed = jax.random.randint(jax.random.fold_in(key, 1), (couples,), 0, 1 << 20) % (room + 1)
    lengths = lengths.at[1:1 + 2 * couples:2].set(giver - passed).at[2:2 + 2 * couples:2].set(taker + passed)
    return lengths[jax.random.permutation(jax.random.fold_in(key, 2), count)]


def centred(own_key, shape, spread, most, cuts=(), kind=jnp.bfloat16):
    level = block_scale(own_key, shape, cuts, -0.22, 0.18) if cuts else 1.0
    entries = jax.random.normal(own_key, shape, jnp.float32) * spread * level
    return jnp.minimum(jnp.maximum(entries, -most), most).astype(kind)


def setup_inputs(seed: int = 0, part: int = 0) -> dict:
    arg_keys = jax.random.split(jax.random.key(seed), 7)
    part_keys = jax.random.split(jax.random.fold_in(arg_keys[6], part), 7)
    return {
        "query": centred(part_keys[0], (TOKENS, H * DK), 1.0, 6.0, ((0, 16),)),
        "key": centred(part_keys[1], (TOKENS, H * DK), 1.0, 6.0, ((0, 16),)),
        "value": centred(part_keys[2], (TOKENS, H * DK), 1.0, 6.0, ((0, 16),)),
        "doc_ids": jnp.searchsorted(jnp.cumsum(uneven_parts(part_keys[3], DOCS, TOKENS, TOKENS // 2, 0)), jnp.arange(TOKENS), side="right").astype(jnp.int32),
        "gates": jnp.clip(jnp.exp(math.log(1.0) - 2.9996462 * jax.random.uniform(part_keys[4], (TOKENS, LEVELS * H), jnp.float32) ** block_scale(part_keys[4], (TOKENS, LEVELS * H), ((0, 16),), -0.2, 0.2)), 0.049804688, 1.0).astype(jnp.bfloat16),
        "gain": jnp.clip(1.0 + 0.1 * jax.random.normal(arg_keys[5], (H * DK,), jnp.float32), 0.5, 1.5),
    }


def bit_levels(count):
    places = jnp.arange(count, dtype=jnp.int32)
    mixed_bits = places[:, None] ^ places[None, :]
    levels = jnp.zeros((count, count), jnp.int32)
    for power in range(count.bit_length()):
        levels = levels + (mixed_bits >= 1 << power).astype(jnp.int32)
    return levels

def local_mix(query, key, value, doc_ids, gates):
    rows = query.shape[0]
    used = rows.bit_length()
    q_heads = query.reshape(rows, H, DK).astype(jnp.float32)
    k_heads = key.reshape(rows, H, DK).astype(jnp.float32)
    v_heads = value.reshape(rows, H, DK).astype(jnp.float32)
    scores = jnp.einsum('thd,shd->hts', q_heads, k_heads)
    levels = bit_levels(rows)
    onehot = (levels[:, :, None] == jnp.arange(used, dtype=jnp.int32)[None, None, :]).astype(jnp.float32)
    table = gates.reshape(rows, LEVELS, H)[:, :used, :].astype(jnp.float32)
    factor = jnp.einsum('tsl,tlh->hts', onehot, table)
    scale = jnp.exp2(-0.5 * levels.astype(jnp.float32))
    places = jnp.arange(rows, dtype=jnp.int32)
    allowed = (places[None, :] <= places[:, None]) & (doc_ids[None, :] == doc_ids[:, None])
    weighted = jnp.where(allowed[None], scores * factor * scale[None], 0.0).astype(jnp.bfloat16)
    return jnp.einsum('hts,shd->thd', weighted.astype(jnp.float32), v_heads)

def run_summary(key, value, doc_ids):
    rows = key.shape[0]
    first_id = doc_ids[0]
    last_id = doc_ids[rows - 1]
    keep = doc_ids == last_id
    kept = jnp.where(keep[:, None], key, jnp.zeros_like(key))
    state = jnp.einsum('thd,the->hde', kept.reshape(rows, H, DK).astype(jnp.float32), value.reshape(rows, H, DK).astype(jnp.float32))
    meta = jnp.stack([first_id, last_id, (first_id == last_id).astype(jnp.int32)])
    return (state, meta)

def reference(query, key, value, doc_ids, gates, gain):
    blocks = N_CTX
    rows = TOK_DEV
    power = rows.bit_length() - 1
    q_blocks = query.reshape(blocks, rows, H * DK)
    k_blocks = key.reshape(blocks, rows, H * DK)
    v_blocks = value.reshape(blocks, rows, H * DK)
    id_blocks = doc_ids.reshape(blocks, rows)
    g_blocks = gates.reshape(blocks, rows, LEVELS * H)
    near = lax.map(lambda items: local_mix(*items), (q_blocks, k_blocks, v_blocks, id_blocks, g_blocks))
    states, metas = jax.vmap(run_summary)(k_blocks, v_blocks, id_blocks)
    q_float = q_blocks.reshape(blocks, rows, H, DK).astype(jnp.float32)
    index = jnp.arange(blocks, dtype=jnp.int32)
    far = jnp.zeros((blocks, rows, H, DK), jnp.float32)
    for bit in range(LOGCTX):
        partner = index ^ 1 << bit
        other_state = states[partner]
        other_meta = metas[partner]
        upper = index >> bit & 1 == 1
        level = power + bit + 1
        valid = (id_blocks == other_meta[:, 1][:, None]) & upper[:, None]
        weight = g_blocks[:, :, level * H:(level + 1) * H].astype(jnp.float32) * 2.0 ** (-0.5 * level)
        weight = jnp.where(valid[:, :, None], weight, 0.0)
        term = jnp.einsum('nthd,nhde->nthe', q_float, other_state, precision=lax.Precision.HIGHEST)
        far = far + weight[:, :, :, None] * term
        low_state = jnp.where(upper[:, None, None, None], other_state, states)
        high_state = jnp.where(upper[:, None, None, None], states, other_state)
        low_meta = jnp.where(upper[:, None], other_meta, metas)
        high_meta = jnp.where(upper[:, None], metas, other_meta)
        joins = (high_meta[:, 2] == 1) & (high_meta[:, 0] == low_meta[:, 1])
        states = high_state + jnp.where(joins[:, None, None, None], low_state, 0.0)
        single = ((low_meta[:, 2] == 1) & joins).astype(jnp.int32)
        metas = jnp.stack([low_meta[:, 0], high_meta[:, 1], single], axis=1)
    attended = near + far
    mean_square = lax.optimization_barrier(jnp.mean(attended * attended, axis=-1, keepdims=True))
    normed = attended * lax.rsqrt(mean_square + 1e-06) * gain.reshape(H, DK)
    return normed.reshape(blocks * rows, H * DK).astype(jnp.bfloat16)
```

```python
import functools
import math

import jax
import jax.numpy as jnp
from jax import lax
from jax.experimental import pallas as pl
from jax.experimental.pallas import tpu as pltpu
from jax.sharding import PartitionSpec as P

H = 16
DK = 128
LEVELS = 16
T = 128
HC = 2
NC = H // HC
HALF = NC // 2
CW = HC * DK
SR = CW + 16
F32 = jnp.float32
BF16 = jnp.bfloat16
R2 = 2.0**-0.5
MESH = pl.DeviceIdType.MESH


def kernel(n, q_hbm, k_hbm, v_hbm, doc_ref, g_ref, gain_ref, out_hbm,
           q, k, v, ost, acc, glo, gm, doct, smask, kmask, loc, mine, sbuf, rbuf,
           ksem, vsem, qsem, osem, send_sem, recv_sem, fwd_sem):
    nb = n.bit_length() - 1
    rows = q.shape[0]
    tiles = rows // T
    me = lax.axis_index("ctx")
    p = lax.rem(me, 2)
    sib = me + 1 - 2 * p

    def partner(b):
        bit = lax.rem(lax.div(me, 2**b), 2)
        return me + (1 - 2 * bit) * 2**b

    def upper(b):
        return lax.rem(lax.div(me, 2**b), 2) == 1

    def cols(c):
        return pl.ds(pl.multiple_of(c * CW, CW), CW)

    def hcols(h):
        return pl.ds(pl.multiple_of(h * DK, DK), DK)

    def load(src, dst, sem, c):
        return pltpu.make_async_copy(src.at[:, cols(c)], dst.at[:, cols(c)], sem.at[c])

    def order(i):
        return lax.rem(lax.div(i, HALF) + 1 - p, 2) * HALF + lax.rem(i, HALF)

    @pl.loop(0, NC)
    def _(i):
        load(k_hbm, k, ksem, order(i)).start()
        load(v_hbm, v, vsem, order(i)).start()

    @pl.loop(0, NC)
    def _(i):
        load(q_hbm, q, qsem, order(i)).start()

    barrier = pltpu.get_barrier_semaphore()
    for b in range(nb):
        pl.semaphore_signal(barrier, inc=1, device_id={"ctx": partner(b)}, device_id_type=MESH)

    it = lax.broadcasted_iota(jnp.int32, (T, T), 0)
    js = lax.broadcasted_iota(jnp.int32, (T, T), 1)
    xo = jnp.bitwise_xor(it, js)
    lev = jnp.zeros((T, T), jnp.int32)
    for power in range(7):
        lev = lev + (xo >= 2**power).astype(jnp.int32)
    scale = jnp.exp2(lev.astype(F32) * -0.5)
    firsts, lasts = [], []
    for j in range(tiles):
        rs = slice(j * T, (j + 1) * T)
        drow = jnp.broadcast_to(doc_ref[j : j + 1, :].astype(F32), (T, T))
        dt = drow.T
        doct[rs, :] = dt
        first, last = dt[0:1, :], dt[T - 1 : T, :]
        firsts.append(first)
        lasts.append(last)
        smask[rs, :] = jnp.where((dt == drow) & (js <= it), scale, 0.0)
        kmask[rs, :] = jnp.where(dt == last, 1.0, 0.0).astype(BF16)
        glo[rs, :] = g_ref[rs, 0:128].astype(F32)
        ghi = g_ref[rs, 128:256].astype(F32)
        if j % 2 == 1:
            gm[0, rs, :] = jnp.where(dt == lasts[j - 1], ghi, 0.0)
        if j >= 2:
            gm[1, rs, :] = jnp.where(dt == lasts[1], ghi, 0.0)

    def joins(hi_first, hi_last, lo_last):
        return jnp.where((hi_first == hi_last) & (hi_first == lo_last), 1.0, 0.0)

    j01 = joins(firsts[1], lasts[1], lasts[0])
    j23 = joins(firsts[3], lasts[3], lasts[2])
    jall = joins(firsts[2], lasts[3], lasts[1])
    rowid = lax.broadcasted_iota(jnp.int32, (16, DK), 0)

    def meta(first, last):
        return jnp.where(rowid == 0, first, last).astype(BF16)

    meta0 = meta(firsts[0], lasts[3])

    pl.semaphore_wait(barrier, nb)

    def send(b, c):
        to = sib if b == 0 else partner(b)
        return pltpu.make_async_remote_copy(
            src_ref=sbuf.at[b, c], dst_ref=rbuf.at[b, c],
            send_sem=send_sem.at[b, c], recv_sem=recv_sem.at[b, c],
            device_id={"ctx": to}, device_id_type=MESH)

    def forward(b, c):
        return pltpu.make_async_remote_copy(
            src_ref=rbuf.at[b, c], dst_ref=rbuf.at[b, c],
            send_sem=fwd_sem.at[b, c], recv_sem=recv_sem.at[b, c],
            device_id={"ctx": sib}, device_id_type=MESH)

    def states(i, own):
        c = order(i)
        load(k_hbm, k, ksem, c).wait()
        load(v_hbm, v, vsem, c).wait()
        for x in range(HC):
            h = c * HC + x
            t = []
            for j in range(tiles):
                rs = slice(j * T, (j + 1) * T)
                km = k[rs, hcols(h)] * kmask[rs, :]
                t.append(lax.dot_general(km, v[rs, hcols(h)], (((0,), (0,)), ((), ())),
                                         preferred_element_type=F32))
            low = t[1] + j01 * t[0]
            high = t[3] + j23 * t[2]
            loc[0, h] = (t[0] * 2.0**-4).astype(BF16)
            loc[1, h] = (t[2] * 2.0**-4).astype(BF16)
            loc[2, h] = (low * 2.0**-4.5).astype(BF16)
            run = (high + jall * low) * 2.0**-5
            if own:
                mine[i - HALF, x * DK : (x + 1) * DK, :] = run
            sbuf[0, c, x * DK : (x + 1) * DK, :] = run.astype(BF16)
        sbuf[0, c, CW:SR, :] = meta0
        send(0, c).start()

    @pl.loop(0, HALF)
    def _(i):
        states(i, False)

    @pl.loop(HALF, NC)
    def _(i):
        states(i, True)

    def step(b, i):
        c = p * HALF + i
        send(b, c).wait_recv()
        if b >= 1:
            forward(b, c).start()
        if b < nb - 1:
            up = upper(b)
            mf = sbuf[b, c, CW:SR, :].astype(F32)
            of = rbuf[b, c, CW:SR, :].astype(F32)
            hi, lo = jnp.where(up, mf, of), jnp.where(up, of, mf)
            join = joins(hi[0:1], hi[1:2], lo[1:2])
            cm, co = jnp.where(up, 1.0, join) * R2, jnp.where(up, join, 1.0) * R2
            merged = mine[i] * cm + rbuf[b, c, 0:CW, :].astype(F32) * co
            mine[i] = merged
            sbuf[b + 1, c, 0:CW, :] = merged.astype(BF16)
            sbuf[b + 1, c, CW:SR, :] = meta(lo[0:1], hi[1:2])
            send(b + 1, c).start()

    lev16 = lev * 16

    def near(c):
        load(q_hbm, q, qsem, c).wait()
        for x in range(HC):
            h = c * HC + x
            idx = lev16 + h
            for j in range(tiles):
                rs = slice(j * T, (j + 1) * T)
                qj = q[rs, hcols(h)]
                s = lax.dot_general(qj, k[rs, hcols(h)], (((1,), (1,)), ((), ())),
                                    preferred_element_type=F32)
                f = jnp.take_along_axis(glo[rs, :], idx, axis=1)
                w = (s * f * smask[rs, :]).astype(BF16)
                o = jnp.dot(w, v[rs, hcols(h)], preferred_element_type=F32)
                if j % 2 == 1:
                    w8 = jnp.take_along_axis(gm[0, rs, :], jnp.full((T, T), h, jnp.int32), axis=1)
                    o = o + w8 * jnp.dot(qj, loc[j // 2, h], preferred_element_type=F32)
                if j >= 2:
                    w9 = jnp.take_along_axis(gm[1, rs, :], jnp.full((T, T), 16 + h, jnp.int32), axis=1)
                    o = o + w9 * jnp.dot(qj, loc[2, h], preferred_element_type=F32)
                acc[rs, hcols(h)] = o

    def weights(b):
        last = rbuf[b, p * HALF, CW:SR, :].astype(F32)[1:2]
        last = jnp.where(upper(b), last, -1.0)
        for j in range(tiles):
            rs = slice(j * T, (j + 1) * T)
            gm[b % 2, rs, :] = jnp.where(doct[rs, :] == last, g_ref[rs, 128:256].astype(F32), 0.0)

    def far(b, c, final):
        for x in range(HC):
            h = c * HC + x
            idx = jnp.full((T, T), (2 + b) * 16 + h, jnp.int32)
            st = rbuf[b, c, x * DK : (x + 1) * DK, :]
            for j in range(tiles):
                rs = slice(j * T, (j + 1) * T)
                w = jnp.take_along_axis(gm[b % 2, rs, :], idx, axis=1)
                a = acc[rs, hcols(h)] + w * jnp.dot(q[rs, hcols(h)], st, preferred_element_type=F32)
                if not final:
                    acc[rs, hcols(h)] = a
                else:
                    ms = jnp.dot((a * a).astype(BF16), jnp.full((DK, DK), 1.0 / DK, BF16),
                                 preferred_element_type=F32)
                    y = a * lax.rsqrt(ms + 1e-6) * gain_ref[:, hcols(h)]
                    ost[rs, hcols(h)] = y.astype(BF16)

    @pl.loop(0, HALF)
    def _(i):
        step(0, i)
        near(p * HALF + i)
        near((1 - p) * HALF + i)

    for b in range(1, nb):
        weights(b - 1)

        @pl.loop(0, HALF)
        def _(i):
            step(b, i)
            far(b - 1, p * HALF + i, False)
            oc = (1 - p) * HALF + i
            send(b - 1, oc).wait_recv()
            far(b - 1, oc, False)

    weights(nb - 1)

    def put(c):
        return pltpu.make_async_copy(ost.at[:, cols(c)], out_hbm.at[:, cols(c)], osem.at[c])

    @pl.loop(0, HALF)
    def _(i):
        c = p * HALF + i
        far(nb - 1, c, True)
        put(c).start()

    @pl.loop(0, HALF)
    def _(i):
        c = (1 - p) * HALF + i
        send(nb - 1, c).wait_recv()
        far(nb - 1, c, True)
        put(c).start()

    @pl.loop(0, NC)
    def _(i):
        send(0, i).wait_send()
        put(i).wait()

    for b in range(1, nb):

        @pl.loop(0, HALF)
        def _(i):
            send(b, p * HALF + i).wait_send()
            forward(b, p * HALF + i).wait_send()


def body(query, key, value, doc_ids, gates, gain):
    n = lax.axis_size("ctx")
    nb = n.bit_length() - 1
    rows, width = query.shape
    hbm = pl.BlockSpec(memory_space=pl.ANY)
    vmem = pl.BlockSpec(memory_space=pltpu.VMEM)
    dma = pltpu.SemaphoreType.DMA
    return pl.pallas_call(
        functools.partial(kernel, n),
        out_shape=jax.ShapeDtypeStruct((rows, width), BF16),
        in_specs=[hbm, hbm, hbm, vmem, vmem, vmem],
        out_specs=hbm,
        scratch_shapes=[
            pltpu.VMEM((rows, width), BF16),
            pltpu.VMEM((rows, width), BF16),
            pltpu.VMEM((rows, width), BF16),
            pltpu.VMEM((rows, width), BF16),
            pltpu.VMEM((rows, width), F32),
            pltpu.VMEM((rows, 128), F32),
            pltpu.VMEM((2, rows, 128), F32),
            pltpu.VMEM((rows, 128), F32),
            pltpu.VMEM((rows, 128), F32),
            pltpu.VMEM((rows, 128), BF16),
            pltpu.VMEM((3, H, DK, DK), BF16),
            pltpu.VMEM((HALF, CW, DK), F32),
            pltpu.VMEM((nb, NC, SR, DK), BF16),
            pltpu.VMEM((nb, NC, SR, DK), BF16),
            dma((NC,)), dma((NC,)), dma((NC,)), dma((NC,)),
            dma((nb, NC)), dma((nb, NC)), dma((nb, NC)),
        ],
        compiler_params=pltpu.CompilerParams(
            collective_id=0, has_side_effects=True, vmem_limit_bytes=56 * 2**20),
    )(query, key, value, doc_ids.reshape(rows // T, T), gates, gain.reshape(1, width))


def solution(mesh):
    placed = (
        P(("grp", "ctx"), None),
        P(("grp", "ctx"), None),
        P(("grp", "ctx"), None),
        P(("grp", "ctx")),
        P(("grp", "ctx"), None),
        P(),
    )
    return jax.shard_map(
        body, mesh=mesh, in_specs=placed, out_specs=P(("grp", "ctx"), None), check_vma=False
    )
```

```python
import functools
import math

import jax
import jax.numpy as jnp
from jax import lax
from jax.experimental import pallas as pl
from jax.experimental.pallas import tpu as pltpu
from jax.sharding import PartitionSpec as P

H = 16
DK = 128
LEVELS = 16
T = 128
HC = 2
NC = H // HC
HALF = NC // 2
CW = HC * DK
HOP = 4
F32 = jnp.float32
BF16 = jnp.bfloat16
R2 = 2.0**-0.5
MESH = pl.DeviceIdType.MESH


def kernel(n, q_hbm, k_hbm, v_hbm, doc_ref, g_ref, gain_ref, out_hbm,
           q, k, v, ost, acc, glo, gm, doct, smask, kmask, loc, mine, coef, sbuf, rbuf,
           smeta, rmeta, ksem, vsem, qsem, osem, send_sem, recv_sem, fwd_sem, msend_sem, mrecv_sem):
    nb = n.bit_length() - 1
    rows = q.shape[0]
    tiles = rows // T
    me = lax.axis_index("ctx")
    p = lax.rem(me, 2)
    sib = me + 1 - 2 * p
    top = nb - 1
    half = n // 2
    above = me >= half
    relay = above & (me + HOP < n)
    source = (me >= half - HOP) & (me < half)
    feeds = jnp.where((me >= half - HOP) & (me + HOP < n), 1, 0)

    def partner(b):
        bit = lax.rem(lax.div(me, 2**b), 2)
        return me + (1 - 2 * bit) * 2**b

    def upper(b):
        return lax.rem(lax.div(me, 2**b), 2) == 1

    def cols(c):
        return pl.ds(pl.multiple_of(c * CW, CW), CW)

    def hcols(h):
        return pl.ds(pl.multiple_of(h * DK, DK), DK)

    def load(src, dst, sem, c):
        return pltpu.make_async_copy(src.at[:, cols(c)], dst.at[:, cols(c)], sem.at[c])

    def order(i):
        return lax.rem(lax.div(i, HALF) + 1 - p, 2) * HALF + lax.rem(i, HALF)

    @pl.loop(0, NC)
    def _(i):
        load(k_hbm, k, ksem, order(i)).start()
        load(v_hbm, v, vsem, order(i)).start()

    @pl.loop(0, NC)
    def _(i):
        load(q_hbm, q, qsem, order(i)).start()

    barrier = pltpu.get_barrier_semaphore()
    for b in range(top):
        pl.semaphore_signal(barrier, inc=1, device_id={"ctx": partner(b)}, device_id_type=MESH)

    @pl.when(above)
    def _():
        pl.semaphore_signal(barrier, inc=1, device_id={"ctx": me - HOP}, device_id_type=MESH)

    @pl.when(jnp.logical_not(above))
    def _():
        rbuf[top] = jnp.zeros_like(rbuf[top])
        rmeta[top] = jnp.zeros_like(rmeta[top])

    it = lax.broadcasted_iota(jnp.int32, (T, T), 0)
    js = lax.broadcasted_iota(jnp.int32, (T, T), 1)
    xo = jnp.bitwise_xor(it, js)
    lev = jnp.zeros((T, T), jnp.int32)
    for power in range(7):
        lev = lev + (xo >= 2**power).astype(jnp.int32)
    scale = jnp.exp2(lev.astype(F32) * -0.5)
    firsts, lasts = [], []
    for j in range(tiles):
        rs = slice(j * T, (j + 1) * T)
        drow = jnp.broadcast_to(doc_ref[j : j + 1, :].astype(F32), (T, T))
        dt = drow.T
        doct[rs, :] = dt
        first, last = dt[0:1, :], dt[T - 1 : T, :]
        firsts.append(first)
        lasts.append(last)
        smask[rs, :] = jnp.where((dt == drow) & (js <= it), scale, 0.0)
        kmask[rs, :] = jnp.where(dt == last, 1.0, 0.0).astype(BF16)
        glo[rs, :] = g_ref[rs, 0:128].astype(F32)
        ghi = g_ref[rs, 128:256].astype(F32)
        if j % 2 == 1:
            gm[0, rs, :] = jnp.where(dt == lasts[j - 1], ghi, 0.0)
        if j >= 2:
            gm[1, rs, :] = jnp.where(dt == lasts[1], ghi, 0.0)

    def joins(hi_first, hi_last, lo_last):
        return jnp.where((hi_first == hi_last) & (hi_first == lo_last), 1.0, 0.0)

    j01 = joins(firsts[1], lasts[1], lasts[0])
    j23 = joins(firsts[3], lasts[3], lasts[2])
    jall = joins(firsts[2], lasts[3], lasts[1])
    rowid = lax.broadcasted_iota(jnp.int32, (16, DK), 0)

    def meta(first, last):
        return jnp.where(rowid == 0, first, last).astype(BF16)

    smeta[0] = meta(firsts[0], lasts[3])

    pl.semaphore_wait(barrier, top + feeds)

    def target(b):
        return sib if b == 0 else partner(b) if b < top else lax.rem(me + HOP, n)

    def remote(src, b, c, sem, to):
        return pltpu.make_async_remote_copy(
            src_ref=src.at[b, c], dst_ref=rbuf.at[b, c],
            send_sem=sem.at[b, c], recv_sem=recv_sem.at[b, c],
            device_id={"ctx": to}, device_id_type=MESH)

    def send(b, c):
        return remote(sbuf, b, c, send_sem, target(b))

    def pass_on(c):
        return remote(rbuf, top, c, send_sem, target(top))

    def forward(b, c):
        return remote(rbuf, b, c, fwd_sem, sib)

    def send_meta(b, src=smeta):
        return pltpu.make_async_remote_copy(
            src_ref=src.at[b], dst_ref=rmeta.at[b],
            send_sem=msend_sem.at[b], recv_sem=mrecv_sem.at[b],
            device_id={"ctx": target(b)}, device_id_type=MESH)

    send_meta(0).start()

    def states(i, own):
        c = order(i)
        load(k_hbm, k, ksem, c).wait()
        load(v_hbm, v, vsem, c).wait()
        for x in range(HC):
            h = c * HC + x
            t = []
            for j in range(tiles):
                rs = slice(j * T, (j + 1) * T)
                km = k[rs, hcols(h)] * kmask[rs, :]
                t.append(lax.dot_general(km, v[rs, hcols(h)], (((0,), (0,)), ((), ())),
                                         preferred_element_type=F32))
            low = t[1] + j01 * t[0]
            high = t[3] + j23 * t[2]
            loc[0, h] = (t[0] * 2.0**-4).astype(BF16)
            loc[1, h] = (t[2] * 2.0**-4).astype(BF16)
            loc[2, h] = (low * 2.0**-4.5).astype(BF16)
            run = (high + jall * low) * 2.0**-5
            if own:
                mine[i - HALF, x * DK : (x + 1) * DK, :] = run
            sbuf[0, c, x * DK : (x + 1) * DK, :] = run.astype(BF16)
        send(0, c).start()

    @pl.loop(0, HALF)
    def _(i):
        states(i, False)

    @pl.loop(HALF, NC)
    def _(i):
        states(i, True)

    def merge_meta(b):
        send_meta(b).wait_recv()
        up = upper(b)
        mf, of = smeta[b].astype(F32), rmeta[b].astype(F32)
        hi, lo = jnp.where(up, mf, of), jnp.where(up, of, mf)
        join = joins(hi[0:1], hi[1:2], lo[1:2])
        coef[b, 0:1, :] = jnp.where(up, 1.0, join) * R2
        coef[b, 1:2, :] = jnp.where(up, join, 1.0) * R2
        smeta[b + 1] = meta(lo[0:1], hi[1:2])
        if b + 1 < top:
            send_meta(b + 1).start()
        else:

            @pl.when(source)
            def _():
                send_meta(top).start()

    def step(b, i):
        c = p * HALF + i
        send(b, c).wait_recv()
        if b >= 1:
            forward(b, c).start()
        merged = mine[i] * coef[b, 0:1, :] + rbuf[b, c].astype(F32) * coef[b, 1:2, :]
        mine[i] = merged
        sbuf[b + 1, c] = merged.astype(BF16)
        if b + 1 < top:
            send(b + 1, c).start()
        else:

            @pl.when(source)
            def _():
                send(top, c).start()

    lev16 = lev * 16

    def near(c):
        load(q_hbm, q, qsem, c).wait()
        for x in range(HC):
            h = c * HC + x
            idx = lev16 + h
            wide = jnp.dot(q[2 * T : 4 * T, hcols(h)], loc[2, h], preferred_element_type=F32)
            for j in range(tiles):
                rs = slice(j * T, (j + 1) * T)
                qj = q[rs, hcols(h)]
                s = lax.dot_general(qj, k[rs, hcols(h)], (((1,), (1,)), ((), ())),
                                    preferred_element_type=F32)
                f = jnp.take_along_axis(glo[rs, :], idx, axis=1)
                w = (s * f * smask[rs, :]).astype(BF16)
                o = jnp.dot(w, v[rs, hcols(h)], preferred_element_type=F32)
                if j % 2 == 1:
                    w8 = jnp.take_along_axis(gm[0, rs, :], jnp.full((T, T), h, jnp.int32), axis=1)
                    o = o + w8 * jnp.dot(qj, loc[j // 2, h], preferred_element_type=F32)
                if j >= 2:
                    js_ = slice((j - 2) * T, (j - 1) * T)
                    w9 = jnp.take_along_axis(gm[1, rs, :], jnp.full((T, T), 16 + h, jnp.int32), axis=1)
                    o = o + w9 * wide[js_, :]
                acc[rs, hcols(h)] = o

    def weights(b):
        last = jnp.where(upper(b), rmeta[b].astype(F32)[1:2], -1.0)
        for j in range(tiles):
            rs = slice(j * T, (j + 1) * T)
            gm[2 + b, rs, :] = jnp.where(doct[rs, :] == last, g_ref[rs, 128:256].astype(F32), 0.0)

    def far(b, c):
        final = b + 1 == top
        for x in range(HC):
            h = c * HC + x
            hs = slice(x * DK, (x + 1) * DK)
            st = jnp.concatenate([rbuf[b, c, hs, :], rbuf[b + 1, c, hs, :]], axis=1)
            m = jnp.dot(q[:, hcols(h)], st, preferred_element_type=F32)
            i0 = jnp.full((T, T), (2 + b) * 16 + h, jnp.int32)
            i1 = i0 + 16
            for j in range(tiles):
                rs = slice(j * T, (j + 1) * T)
                w0 = jnp.take_along_axis(gm[2 + b, rs, :], i0, axis=1)
                w1 = jnp.take_along_axis(gm[3 + b, rs, :], i1, axis=1)
                a = acc[rs, hcols(h)] + w0 * m[rs, 0:DK] + w1 * m[rs, DK : 2 * DK]
                if not final:
                    acc[rs, hcols(h)] = a
                else:
                    ms = jnp.dot((a * a).astype(BF16), jnp.full((DK, DK), 1.0 / DK, BF16),
                                 preferred_element_type=F32)
                    y = a * lax.rsqrt(ms + 1e-6) * gain_ref[:, hcols(h)]
                    ost[rs, hcols(h)] = y.astype(BF16)

    def put(c):
        return pltpu.make_async_copy(ost.at[:, cols(c)], out_hbm.at[:, cols(c)], osem.at[c])

    merge_meta(0)

    @pl.loop(0, HALF)
    def _(i):
        step(0, i)

    weights(0)
    merge_meta(1)

    @pl.loop(0, HALF)
    def _(i):
        near(p * HALF + i)
        near((1 - p) * HALF + i)
        step(1, i)

    weights(1)
    for b in range(2, top):
        merge_meta(b)

        @pl.loop(0, HALF)
        def _(i):
            step(b, i)
            if b % 2 == 0:
                oc = (1 - p) * HALF + i
                if b == 2:
                    send(0, oc).wait_recv()
                far(b - 2, p * HALF + i)
                send(b - 1, oc).wait_recv()
                far(b - 2, oc)
            else:
                send(b - 1, (1 - p) * HALF + i).wait_recv()

        weights(b)

    @pl.when(above)
    def _():
        send_meta(top).wait_recv()

    @pl.when(relay)
    def _():
        send_meta(top, rmeta).start()

        @pl.loop(0, HALF)
        def _(i):
            c = p * HALF + i
            send(top, c).wait_recv()
            pass_on(c).start()
            forward(top, c).start()

    weights(top)

    def rest(i):
        oc = (1 - p) * HALF + i
        send(top - 1, oc).wait_recv()

        @pl.when(above)
        def _():
            send(top, oc).wait_recv()

        far(top - 1, oc)
        put(oc).start()

    @pl.loop(0, HALF + 1)
    def _(i):
        @pl.when(i < HALF)
        def _():
            c = p * HALF + i

            @pl.when(above & jnp.logical_not(relay))
            def _():
                send(top, c).wait_recv()
                forward(top, c).start()

            far(top - 1, c)
            put(c).start()

        @pl.when(i > 0)
        def _():
            rest(i - 1)

    @pl.loop(0, NC)
    def _(i):
        send(0, i).wait_send()
        put(i).wait()

    for b in range(top):
        send_meta(b).wait_send()

    for b in range(1, top):

        @pl.loop(0, HALF)
        def _(i):
            send(b, p * HALF + i).wait_send()
            forward(b, p * HALF + i).wait_send()

    @pl.when(feeds == 1)
    def _():
        send_meta(top).wait_send()

        @pl.loop(0, HALF)
        def _(i):
            send(top, p * HALF + i).wait_send()

    @pl.when(above)
    def _():
        @pl.loop(0, HALF)
        def _(i):
            forward(top, p * HALF + i).wait_send()


def body(query, key, value, doc_ids, gates, gain):
    n = lax.axis_size("ctx")
    nb = n.bit_length() - 1
    rows, width = query.shape
    hbm = pl.BlockSpec(memory_space=pl.ANY)
    vmem = pl.BlockSpec(memory_space=pltpu.VMEM)
    dma = pltpu.SemaphoreType.DMA
    return pl.pallas_call(
        functools.partial(kernel, n),
        out_shape=jax.ShapeDtypeStruct((rows, width), BF16),
        in_specs=[hbm, hbm, hbm, vmem, vmem, vmem],
        out_specs=hbm,
        scratch_shapes=[
            pltpu.VMEM((rows, width), BF16),
            pltpu.VMEM((rows, width), BF16),
            pltpu.VMEM((rows, width), BF16),
            pltpu.VMEM((rows, width), BF16),
            pltpu.VMEM((rows, width), F32),
            pltpu.VMEM((rows, 128), F32),
            pltpu.VMEM((2 + nb, rows, 128), F32),
            pltpu.VMEM((rows, 128), F32),
            pltpu.VMEM((rows, 128), F32),
            pltpu.VMEM((rows, 128), BF16),
            pltpu.VMEM((3, H, DK, DK), BF16),
            pltpu.VMEM((HALF, CW, DK), F32),
            pltpu.VMEM((nb, 8, DK), F32),
            pltpu.VMEM((nb, NC, CW, DK), BF16),
            pltpu.VMEM((nb, NC, CW, DK), BF16),
            pltpu.VMEM((nb, 16, DK), BF16),
            pltpu.VMEM((nb, 16, DK), BF16),
            dma((NC,)), dma((NC,)), dma((NC,)), dma((NC,)),
            dma((nb, NC)), dma((nb, NC)), dma((nb, NC)), dma((nb,)), dma((nb,)),
        ],
        compiler_params=pltpu.CompilerParams(
            collective_id=0, has_side_effects=True, vmem_limit_bytes=56 * 2**20),
    )(query, key, value, doc_ids.reshape(rows // T, T), gates, gain.reshape(1, width))


def solution(mesh):
    placed = (
        P(("grp", "ctx"), None),
        P(("grp", "ctx"), None),
        P(("grp", "ctx"), None),
        P(("grp", "ctx")),
        P(("grp", "ctx"), None),
        P(),
    )
    return jax.shard_map(
        body, mesh=mesh, in_specs=placed, out_specs=P(("grp", "ctx"), None), check_vma=False
    )
```

```python
import functools
import math

import jax
import jax.numpy as jnp
from jax import lax
from jax.experimental import pallas as pl
from jax.experimental.pallas import tpu as pltpu
from jax.sharding import PartitionSpec as P

H = 16
DK = 128
LEVELS = 16
T = 128
HC = 2
NC = H // HC
HALF = NC // 2
CW = HC * DK
HOP = 4
F32 = jnp.float32
BF16 = jnp.bfloat16
R2 = 2.0**-0.5
MESH = pl.DeviceIdType.MESH


def kernel(n, q_hbm, k_hbm, v_hbm, doc_ref, g_ref, gain_ref, ost,
           q, k, v, acc, glo, gm, doct, smask, kmask, loc, mine, coef, sbuf, rbuf,
           smeta, rmeta, ksem, vsem, qsem, send_sem, recv_sem, fwd_sem, msend_sem, mrecv_sem):
    nb = n.bit_length() - 1
    rows = q.shape[0]
    tiles = rows // T
    me = lax.axis_index("ctx")
    p = lax.rem(me, 2)
    sib = me + 1 - 2 * p
    top = nb - 1
    half = n // 2
    above = me >= half
    relay = above & (me + HOP < n)
    source = (me >= half - HOP) & (me < half)
    feeds = jnp.where((me >= half - HOP) & (me + HOP < n), 1, 0)

    def partner(b):
        bit = lax.rem(lax.div(me, 2**b), 2)
        return me + (1 - 2 * bit) * 2**b

    def upper(b):
        return lax.rem(lax.div(me, 2**b), 2) == 1

    def cols(c):
        return pl.ds(pl.multiple_of(c * CW, CW), CW)

    def hcols(h):
        return pl.ds(pl.multiple_of(h * DK, DK), DK)

    def load(src, dst, sem, c):
        return pltpu.make_async_copy(src.at[:, cols(c)], dst.at[:, cols(c)], sem.at[c])

    def order(i):
        return lax.rem(lax.div(i, HALF) + 1 - p, 2) * HALF + lax.rem(i, HALF)

    @pl.loop(0, NC)
    def _(i):
        load(k_hbm, k, ksem, order(i)).start()
        load(v_hbm, v, vsem, order(i)).start()

    @pl.loop(0, NC)
    def _(i):
        load(q_hbm, q, qsem, order(i)).start()

    barrier = pltpu.get_barrier_semaphore()
    for b in range(top):
        pl.semaphore_signal(barrier, inc=1, device_id={"ctx": partner(b)}, device_id_type=MESH)

    @pl.when(above)
    def _():
        pl.semaphore_signal(barrier, inc=1, device_id={"ctx": me - HOP}, device_id_type=MESH)

    @pl.when(jnp.logical_not(above))
    def _():
        rbuf[top] = jnp.zeros_like(rbuf[top])
        rmeta[top] = jnp.zeros_like(rmeta[top])

    it = lax.broadcasted_iota(jnp.int32, (T, T), 0)
    js = lax.broadcasted_iota(jnp.int32, (T, T), 1)
    xo = jnp.bitwise_xor(it, js)
    lev = jnp.zeros((T, T), jnp.int32)
    for power in range(7):
        lev = lev + (xo >= 2**power).astype(jnp.int32)
    scale = jnp.exp2(lev.astype(F32) * -0.5)
    firsts, lasts = [], []
    for j in range(tiles):
        rs = slice(j * T, (j + 1) * T)
        drow = jnp.broadcast_to(doc_ref[j : j + 1, :].astype(F32), (T, T))
        dt = drow.T
        doct[rs, :] = dt
        first, last = dt[0:1, :], dt[T - 1 : T, :]
        firsts.append(first)
        lasts.append(last)
        smask[rs, :] = jnp.where((dt == drow) & (js <= it), scale, 0.0)
        kmask[rs, :] = jnp.where(dt == last, 1.0, 0.0).astype(BF16)
        glo[rs, :] = g_ref[rs, 0:128].astype(F32)
        ghi = g_ref[rs, 128:256].astype(F32)
        if j % 2 == 1:
            gm[0, rs, :] = jnp.where(dt == lasts[j - 1], ghi, 0.0)
        if j >= 2:
            gm[1, rs, :] = jnp.where(dt == lasts[1], ghi, 0.0)

    def joins(hi_first, hi_last, lo_last):
        return jnp.where((hi_first == hi_last) & (hi_first == lo_last), 1.0, 0.0)

    j01 = joins(firsts[1], lasts[1], lasts[0])
    j23 = joins(firsts[3], lasts[3], lasts[2])
    jall = joins(firsts[2], lasts[3], lasts[1])
    rowid = lax.broadcasted_iota(jnp.int32, (16, DK), 0)

    def meta(first, last):
        return jnp.where(rowid == 0, first, last).astype(BF16)

    smeta[0] = meta(firsts[0], lasts[3])

    pl.semaphore_wait(barrier, top + feeds)

    def target(b):
        return sib if b == 0 else partner(b) if b < top else lax.rem(me + HOP, n)

    def remote(src, b, c, sem, to):
        return pltpu.make_async_remote_copy(
            src_ref=src.at[b, c], dst_ref=rbuf.at[b, c],
            send_sem=sem.at[b, c], recv_sem=recv_sem.at[b, c],
            device_id={"ctx": to}, device_id_type=MESH)

    def send(b, c):
        return remote(sbuf, b, c, send_sem, target(b))

    def pass_on(c):
        return remote(rbuf, top, c, send_sem, target(top))

    def forward(b, c):
        return remote(rbuf, b, c, fwd_sem, sib)

    def send_meta(b, src=smeta):
        return pltpu.make_async_remote_copy(
            src_ref=src.at[b], dst_ref=rmeta.at[b],
            send_sem=msend_sem.at[b], recv_sem=mrecv_sem.at[b],
            device_id={"ctx": target(b)}, device_id_type=MESH)

    send_meta(0).start()

    def states(i, own):
        c = order(i)
        load(k_hbm, k, ksem, c).wait()
        load(v_hbm, v, vsem, c).wait()
        for x in range(HC):
            h = c * HC + x
            t = []
            for j in range(tiles):
                rs = slice(j * T, (j + 1) * T)
                km = k[rs, hcols(h)] * kmask[rs, :]
                t.append(lax.dot_general(km, v[rs, hcols(h)], (((0,), (0,)), ((), ())),
                                         preferred_element_type=F32))
            low = t[1] + j01 * t[0]
            high = t[3] + j23 * t[2]
            loc[0, h] = (t[0] * 2.0**-4).astype(BF16)
            loc[1, h] = (t[2] * 2.0**-4).astype(BF16)
            loc[2, h] = (low * 2.0**-4.5).astype(BF16)
            run = (high + jall * low) * 2.0**-5
            if own:
                mine[i - HALF, x * DK : (x + 1) * DK, :] = run
            sbuf[0, c, x * DK : (x + 1) * DK, :] = run.astype(BF16)
        send(0, c).start()

    @pl.loop(0, HALF)
    def _(i):
        states(i, False)

    @pl.loop(HALF, NC)
    def _(i):
        states(i, True)

    def merge_meta(b):
        send_meta(b).wait_recv()
        up = upper(b)
        mf, of = smeta[b].astype(F32), rmeta[b].astype(F32)
        hi, lo = jnp.where(up, mf, of), jnp.where(up, of, mf)
        join = joins(hi[0:1], hi[1:2], lo[1:2])
        coef[b, 0:1, :] = jnp.where(up, 1.0, join) * R2
        coef[b, 1:2, :] = jnp.where(up, join, 1.0) * R2
        smeta[b + 1] = meta(lo[0:1], hi[1:2])
        if b + 1 < top:
            send_meta(b + 1).start()
        else:

            @pl.when(source)
            def _():
                send_meta(top).start()

    def step(b, i):
        c = p * HALF + i
        send(b, c).wait_recv()
        if b >= 1:
            forward(b, c).start()
        merged = mine[i] * coef[b, 0:1, :] + rbuf[b, c].astype(F32) * coef[b, 1:2, :]
        mine[i] = merged
        sbuf[b + 1, c] = merged.astype(BF16)
        if b + 1 < top:
            send(b + 1, c).start()
        else:

            @pl.when(source)
            def _():
                send(top, c).start()

    lev16 = lev * 16

    def near(c):
        load(q_hbm, q, qsem, c).wait()
        for x in range(HC):
            h = c * HC + x
            idx = lev16 + h
            wide = jnp.dot(q[2 * T : 4 * T, hcols(h)], loc[2, h], preferred_element_type=F32)
            for j in range(tiles):
                rs = slice(j * T, (j + 1) * T)
                qj = q[rs, hcols(h)]
                s = lax.dot_general(qj, k[rs, hcols(h)], (((1,), (1,)), ((), ())),
                                    preferred_element_type=F32)
                f = jnp.take_along_axis(glo[rs, :], idx, axis=1)
                w = (s * f * smask[rs, :]).astype(BF16)
                o = jnp.dot(w, v[rs, hcols(h)], preferred_element_type=F32)
                if j % 2 == 1:
                    w8 = jnp.take_along_axis(gm[0, rs, :], jnp.full((T, T), h, jnp.int32), axis=1)
                    o = o + w8 * jnp.dot(qj, loc[j // 2, h], preferred_element_type=F32)
                if j >= 2:
                    js_ = slice((j - 2) * T, (j - 1) * T)
                    w9 = jnp.take_along_axis(gm[1, rs, :], jnp.full((T, T), 16 + h, jnp.int32), axis=1)
                    o = o + w9 * wide[js_, :]
                acc[rs, hcols(h)] = o

    def weights(b):
        last = jnp.where(upper(b), rmeta[b].astype(F32)[1:2], -1.0)
        for j in range(tiles):
            rs = slice(j * T, (j + 1) * T)
            gm[2 + b, rs, :] = jnp.where(doct[rs, :] == last, g_ref[rs, 128:256].astype(F32), 0.0)

    def far(b, c):
        final = b + 1 == top
        for x in range(HC):
            h = c * HC + x
            hs = slice(x * DK, (x + 1) * DK)
            st = jnp.concatenate([rbuf[b, c, hs, :], rbuf[b + 1, c, hs, :]], axis=1)
            m = jnp.dot(q[:, hcols(h)], st, preferred_element_type=F32)
            i0 = jnp.full((T, T), (2 + b) * 16 + h, jnp.int32)
            i1 = i0 + 16
            for j in range(tiles):
                rs = slice(j * T, (j + 1) * T)
                w0 = jnp.take_along_axis(gm[2 + b, rs, :], i0, axis=1)
                w1 = jnp.take_along_axis(gm[3 + b, rs, :], i1, axis=1)
                a = acc[rs, hcols(h)] + w0 * m[rs, 0:DK] + w1 * m[rs, DK : 2 * DK]
                if not final:
                    acc[rs, hcols(h)] = a
                else:
                    ms = jnp.dot((a * a).astype(BF16), jnp.full((DK, DK), 1.0 / DK, BF16),
                                 preferred_element_type=F32)
                    y = a * lax.rsqrt(ms + 1e-6) * gain_ref[:, hcols(h)]
                    ost[rs, hcols(h)] = y.astype(BF16)

    merge_meta(0)

    @pl.loop(0, HALF)
    def _(i):
        step(0, i)

    weights(0)
    merge_meta(1)

    @pl.loop(0, HALF)
    def _(i):
        near(p * HALF + i)
        near((1 - p) * HALF + i)
        step(1, i)

    weights(1)
    for b in range(2, top):
        merge_meta(b)

        @pl.loop(0, HALF)
        def _(i):
            step(b, i)
            if b % 2 == 0:
                oc = (1 - p) * HALF + i
                if b == 2:
                    send(0, oc).wait_recv()
                far(b - 2, p * HALF + i)
                send(b - 1, oc).wait_recv()
                far(b - 2, oc)
            else:
                send(b - 1, (1 - p) * HALF + i).wait_recv()

        weights(b)

    @pl.when(above)
    def _():
        send_meta(top).wait_recv()

    @pl.when(relay)
    def _():
        send_meta(top, rmeta).start()

        @pl.loop(0, HALF)
        def _(i):
            c = p * HALF + i
            send(top, c).wait_recv()
            pass_on(c).start()
            forward(top, c).start()

    weights(top)

    def rest(i):
        oc = (1 - p) * HALF + i
        send(top - 1, oc).wait_recv()

        @pl.when(above)
        def _():
            send(top, oc).wait_recv()

        far(top - 1, oc)

    @pl.loop(0, HALF + 1)
    def _(i):
        @pl.when(i < HALF)
        def _():
            c = p * HALF + i

            @pl.when(above & jnp.logical_not(relay))
            def _():
                send(top, c).wait_recv()
                forward(top, c).start()

            far(top - 1, c)

        @pl.when(i > 0)
        def _():
            rest(i - 1)

    @pl.loop(0, NC)
    def _(i):
        send(0, i).wait_send()

    for b in range(top):
        send_meta(b).wait_send()

    for b in range(1, top):

        @pl.loop(0, HALF)
        def _(i):
            send(b, p * HALF + i).wait_send()
            forward(b, p * HALF + i).wait_send()

    @pl.when(feeds == 1)
    def _():
        send_meta(top).wait_send()

        @pl.loop(0, HALF)
        def _(i):
            send(top, p * HALF + i).wait_send()

    @pl.when(above)
    def _():
        @pl.loop(0, HALF)
        def _(i):
            forward(top, p * HALF + i).wait_send()


def body(query, key, value, doc_ids, gates, gain):
    n = lax.axis_size("ctx")
    nb = n.bit_length() - 1
    rows, width = query.shape
    hbm = pl.BlockSpec(memory_space=pltpu.HBM)
    vmem = pl.BlockSpec(memory_space=pltpu.VMEM)
    dma = pltpu.SemaphoreType.DMA
    return pl.pallas_call(
        functools.partial(kernel, n),
        out_shape=pltpu.VMEM((rows, width), BF16),
        in_specs=[hbm, hbm, hbm, vmem, vmem, vmem],
        out_specs=vmem,
        scratch_shapes=[
            pltpu.VMEM((rows, width), BF16),
            pltpu.VMEM((rows, width), BF16),
            pltpu.VMEM((rows, width), BF16),
            pltpu.VMEM((rows, width), F32),
            pltpu.VMEM((rows, 128), F32),
            pltpu.VMEM((2 + nb, rows, 128), F32),
            pltpu.VMEM((rows, 128), F32),
            pltpu.VMEM((rows, 128), F32),
            pltpu.VMEM((rows, 128), BF16),
            pltpu.VMEM((3, H, DK, DK), BF16),
            pltpu.VMEM((HALF, CW, DK), F32),
            pltpu.VMEM((nb, 8, DK), F32),
            pltpu.VMEM((nb, NC, CW, DK), BF16),
            pltpu.VMEM((nb, NC, CW, DK), BF16),
            pltpu.VMEM((nb, 16, DK), BF16),
            pltpu.VMEM((nb, 16, DK), BF16),
            dma((NC,)), dma((NC,)), dma((NC,)),
            dma((nb, NC)), dma((nb, NC)), dma((nb, NC)), dma((nb,)), dma((nb,)),
        ],
        compiler_params=pltpu.CompilerParams(
            collective_id=0, has_side_effects=True, vmem_limit_bytes=58 * 2**20),
    )(query, key, value, doc_ids.reshape(rows // T, T), gates, gain.reshape(1, width))


def solution(mesh):
    placed = (
        P(("grp", "ctx"), None),
        P(("grp", "ctx"), None),
        P(("grp", "ctx"), None),
        P(("grp", "ctx")),
        P(("grp", "ctx"), None),
        P(),
    )
    return jax.shard_map(
        body, mesh=mesh, in_specs=placed, out_specs=P(("grp", "ctx"), None), check_vma=False
    )
```

```python
import functools
import math

import jax
import jax.numpy as jnp
from jax import lax
from jax.experimental import pallas as pl
from jax.experimental.pallas import tpu as pltpu
from jax.sharding import PartitionSpec as P

H = 16
DK = 128
LEVELS = 16
T = 128
HC = 2
NC = H // HC
HALF = NC // 2
CW = HC * DK
HOP = 4
F32 = jnp.float32
BF16 = jnp.bfloat16
R2 = 2.0**-0.5
MESH = pl.DeviceIdType.MESH


def kernel(n, q_hbm, k_hbm, v_hbm, doc_ref, g_ref, gain_ref, ost,
           q, k, v, acc, glo, gm, doct, smask, kmask, loc, mine, coef, sbuf, rbuf,
           smeta, rmeta, ksem, vsem, qsem, send_sem, recv_sem, fwd_sem, msend_sem, mrecv_sem):
    nb = n.bit_length() - 1
    rows = q.shape[0]
    tiles = rows // T
    me = lax.axis_index("ctx")
    p = lax.rem(me, 2)
    sib = me + 1 - 2 * p
    top = nb - 1
    half = n // 2
    above = me >= half
    relay = above & (me + HOP < n)
    source = (me >= half - HOP) & (me < half)
    feeds = jnp.where((me >= half - HOP) & (me + HOP < n), 1, 0)

    def partner(b):
        bit = lax.rem(lax.div(me, 2**b), 2)
        return me + (1 - 2 * bit) * 2**b

    def upper(b):
        return lax.rem(lax.div(me, 2**b), 2) == 1

    def cols(c):
        return pl.ds(pl.multiple_of(c * CW, CW), CW)

    def hcols(h):
        return pl.ds(pl.multiple_of(h * DK, DK), DK)

    def load(src, dst, sem, c):
        return pltpu.make_async_copy(src.at[:, cols(c)], dst.at[:, cols(c)], sem.at[c])

    def order(i):
        return lax.rem(lax.div(i, HALF) + 1 - p, 2) * HALF + lax.rem(i, HALF)

    @pl.loop(0, NC)
    def _(i):
        load(k_hbm, k, ksem, order(i)).start()
        load(v_hbm, v, vsem, order(i)).start()

    @pl.loop(0, NC)
    def _(i):
        load(q_hbm, q, qsem, order(i)).start()

    barrier = pltpu.get_barrier_semaphore()
    for b in range(top):
        pl.semaphore_signal(barrier, inc=1, device_id={"ctx": partner(b)}, device_id_type=MESH)

    @pl.when(above)
    def _():
        pl.semaphore_signal(barrier, inc=1, device_id={"ctx": me - HOP}, device_id_type=MESH)

    @pl.when(jnp.logical_not(above))
    def _():
        rbuf[top] = jnp.zeros_like(rbuf[top])
        rmeta[top] = jnp.zeros_like(rmeta[top])

    it = lax.broadcasted_iota(jnp.int32, (T, T), 0)
    js = lax.broadcasted_iota(jnp.int32, (T, T), 1)
    xo = jnp.bitwise_xor(it, js)
    lev = jnp.zeros((T, T), jnp.int32)
    for power in range(7):
        lev = lev + (xo >= 2**power).astype(jnp.int32)
    scale = jnp.exp2(lev.astype(F32) * -0.5)
    firsts, lasts = [], []
    for j in range(tiles):
        rs = slice(j * T, (j + 1) * T)
        drow = jnp.broadcast_to(doc_ref[j : j + 1, :].astype(F32), (T, T))
        dt = drow.T
        doct[rs, :] = dt
        first, last = dt[0:1, :], dt[T - 1 : T, :]
        firsts.append(first)
        lasts.append(last)
        smask[rs, :] = jnp.where((dt == drow) & (js <= it), scale, 0.0)
        kmask[rs, :] = jnp.where(dt == last, 1.0, 0.0).astype(BF16)
        glo[rs, :] = g_ref[rs, 0:128].astype(F32)
        ghi = g_ref[rs, 128:256].astype(F32)
        if j % 2 == 1:
            gm[0, rs, :] = jnp.where(dt == lasts[j - 1], ghi, 0.0)
        if j >= 2:
            gm[1, rs, :] = jnp.where(dt == lasts[1], ghi, 0.0)

    def joins(hi_first, hi_last, lo_last):
        return jnp.where((hi_first == hi_last) & (hi_first == lo_last), 1.0, 0.0)

    j01 = joins(firsts[1], lasts[1], lasts[0])
    j23 = joins(firsts[3], lasts[3], lasts[2])
    jall = joins(firsts[2], lasts[3], lasts[1])
    rowid = lax.broadcasted_iota(jnp.int32, (16, DK), 0)

    def meta(first, last):
        return jnp.where(rowid == 0, first, last).astype(BF16)

    smeta[0] = meta(firsts[0], lasts[3])

    pl.semaphore_wait(barrier, top + feeds)

    def target(b):
        return sib if b == 0 else partner(b) if b < top else lax.rem(me + HOP, n)

    def remote(src, b, c, sem, to):
        return pltpu.make_async_remote_copy(
            src_ref=src.at[b, c], dst_ref=rbuf.at[b, c],
            send_sem=sem.at[b, c], recv_sem=recv_sem.at[b, c],
            device_id={"ctx": to}, device_id_type=MESH)

    def send(b, c):
        return remote(sbuf, b, c, send_sem, target(b))

    def pass_on(c):
        return remote(rbuf, top, c, send_sem, target(top))

    def forward(b, c):
        return remote(rbuf, b, c, fwd_sem, sib)

    def send_meta(b, src=smeta):
        return pltpu.make_async_remote_copy(
            src_ref=src.at[b], dst_ref=rmeta.at[b],
            send_sem=msend_sem.at[b], recv_sem=mrecv_sem.at[b],
            device_id={"ctx": target(b)}, device_id_type=MESH)

    send_meta(0).start()

    def states(i, own):
        c = order(i)
        load(k_hbm, k, ksem, c).wait()
        load(v_hbm, v, vsem, c).wait()
        for x in range(HC):
            h = c * HC + x
            t = []
            for j in range(tiles):
                rs = slice(j * T, (j + 1) * T)
                km = k[rs, hcols(h)] * kmask[rs, :]
                t.append(lax.dot_general(km, v[rs, hcols(h)], (((0,), (0,)), ((), ())),
                                         preferred_element_type=F32))
            low = t[1] + j01 * t[0]
            high = t[3] + j23 * t[2]
            loc[0, h] = (t[0] * 2.0**-4).astype(BF16)
            loc[1, h] = (t[2] * 2.0**-4).astype(BF16)
            loc[2, h] = (low * 2.0**-4.5).astype(BF16)
            run = (high + jall * low) * 2.0**-5
            if own:
                mine[i - HALF, x * DK : (x + 1) * DK, :] = run
            sbuf[0, c, x * DK : (x + 1) * DK, :] = run.astype(BF16)
        send(0, c).start()

    @pl.loop(0, HALF)
    def _(i):
        states(i, False)

    def merge_meta(b):
        send_meta(b).wait_recv()
        up = upper(b)
        mf, of = smeta[b].astype(F32), rmeta[b].astype(F32)
        hi, lo = jnp.where(up, mf, of), jnp.where(up, of, mf)
        join = joins(hi[0:1], hi[1:2], lo[1:2])
        coef[b, 0:1, :] = jnp.where(up, 1.0, join) * R2
        coef[b, 1:2, :] = jnp.where(up, join, 1.0) * R2
        smeta[b + 1] = meta(lo[0:1], hi[1:2])
        if b + 1 < top:
            send_meta(b + 1).start()
        else:

            @pl.when(source)
            def _():
                send_meta(top).start()

    def step(b, i):
        c = p * HALF + i
        send(b, c).wait_recv()
        if b >= 1:
            forward(b, c).start()
        merged = mine[i] * coef[b, 0:1, :] + rbuf[b, c].astype(F32) * coef[b, 1:2, :]
        mine[i] = merged
        sbuf[b + 1, c] = merged.astype(BF16)
        if b + 1 < top:
            send(b + 1, c).start()
        else:

            @pl.when(source)
            def _():
                send(top, c).start()

    lev16 = lev * 16

    def near(c):
        load(q_hbm, q, qsem, c).wait()
        for x in range(HC):
            h = c * HC + x
            idx = lev16 + h
            wide = jnp.dot(q[2 * T : 4 * T, hcols(h)], loc[2, h], preferred_element_type=F32)
            for j in range(tiles):
                rs = slice(j * T, (j + 1) * T)
                qj = q[rs, hcols(h)]
                s = lax.dot_general(qj, k[rs, hcols(h)], (((1,), (1,)), ((), ())),
                                    preferred_element_type=F32)
                f = jnp.take_along_axis(glo[rs, :], idx, axis=1)
                w = (s * f * smask[rs, :]).astype(BF16)
                o = jnp.dot(w, v[rs, hcols(h)], preferred_element_type=F32)
                if j % 2 == 1:
                    w8 = jnp.take_along_axis(gm[0, rs, :], jnp.full((T, T), h, jnp.int32), axis=1)
                    o = o + w8 * jnp.dot(qj, loc[j // 2, h], preferred_element_type=F32)
                if j >= 2:
                    js_ = slice((j - 2) * T, (j - 1) * T)
                    w9 = jnp.take_along_axis(gm[1, rs, :], jnp.full((T, T), 16 + h, jnp.int32), axis=1)
                    o = o + w9 * wide[js_, :]
                acc[rs, hcols(h)] = o

    def weights(b):
        last = jnp.where(upper(b), rmeta[b].astype(F32)[1:2], -1.0)
        for j in range(tiles):
            rs = slice(j * T, (j + 1) * T)
            gm[2 + b, rs, :] = jnp.where(doct[rs, :] == last, g_ref[rs, 128:256].astype(F32), 0.0)

    def far(b, c):
        final = b + 1 == top
        for x in range(HC):
            h = c * HC + x
            hs = slice(x * DK, (x + 1) * DK)
            st = jnp.concatenate([rbuf[b, c, hs, :], rbuf[b + 1, c, hs, :]], axis=1)
            m = jnp.dot(q[:, hcols(h)], st, preferred_element_type=F32)
            i0 = jnp.full((T, T), (2 + b) * 16 + h, jnp.int32)
            i1 = i0 + 16
            for j in range(tiles):
                rs = slice(j * T, (j + 1) * T)
                w0 = jnp.take_along_axis(gm[2 + b, rs, :], i0, axis=1)
                w1 = jnp.take_along_axis(gm[3 + b, rs, :], i1, axis=1)
                a = acc[rs, hcols(h)] + w0 * m[rs, 0:DK] + w1 * m[rs, DK : 2 * DK]
                if not final:
                    acc[rs, hcols(h)] = a
                else:
                    ms = jnp.dot((a * a).astype(BF16), jnp.full((DK, DK), 1.0 / DK, BF16),
                                 preferred_element_type=F32)
                    y = a * lax.rsqrt(ms + 1e-6) * gain_ref[:, hcols(h)]
                    ost[rs, hcols(h)] = y.astype(BF16)

    merge_meta(0)

    @pl.loop(0, HALF)
    def _(i):
        states(i + HALF, True)
        step(0, i)

    weights(0)
    merge_meta(1)

    @pl.loop(0, HALF)
    def _(i):
        near(p * HALF + i)
        near((1 - p) * HALF + i)
        step(1, i)

    weights(1)
    for b in range(2, top):
        merge_meta(b)

        @pl.loop(0, HALF)
        def _(i):
            step(b, i)
            if b % 2 == 0:
                oc = (1 - p) * HALF + i
                if b == 2:
                    send(0, oc).wait_recv()
                far(b - 2, p * HALF + i)
                send(b - 1, oc).wait_recv()
                far(b - 2, oc)
            else:
                send(b - 1, (1 - p) * HALF + i).wait_recv()

        weights(b)

    @pl.when(above)
    def _():
        send_meta(top).wait_recv()

    @pl.when(relay)
    def _():
        send_meta(top, rmeta).start()

        @pl.loop(0, HALF)
        def _(i):
            c = p * HALF + i
            send(top, c).wait_recv()
            pass_on(c).start()
            forward(top, c).start()

    weights(top)

    def rest(i):
        oc = (1 - p) * HALF + i
        send(top - 1, oc).wait_recv()

        @pl.when(above)
        def _():
            send(top, oc).wait_recv()

        far(top - 1, oc)

    @pl.loop(0, HALF + 1)
    def _(i):
        @pl.when(i < HALF)
        def _():
            c = p * HALF + i

            @pl.when(above & jnp.logical_not(relay))
            def _():
                send(top, c).wait_recv()
                forward(top, c).start()

            far(top - 1, c)

        @pl.when(i > 0)
        def _():
            rest(i - 1)

    @pl.loop(0, NC)
    def _(i):
        send(0, i).wait_send()

    for b in range(top):
        send_meta(b).wait_send()

    for b in range(1, top):

        @pl.loop(0, HALF)
        def _(i):
            send(b, p * HALF + i).wait_send()
            forward(b, p * HALF + i).wait_send()

    @pl.when(feeds == 1)
    def _():
        send_meta(top).wait_send()

        @pl.loop(0, HALF)
        def _(i):
            send(top, p * HALF + i).wait_send()

    @pl.when(above)
    def _():
        @pl.loop(0, HALF)
        def _(i):
            forward(top, p * HALF + i).wait_send()


def body(query, key, value, doc_ids, gates, gain):
    n = lax.axis_size("ctx")
    nb = n.bit_length() - 1
    rows, width = query.shape
    hbm = pl.BlockSpec(memory_space=pltpu.HBM)
    vmem = pl.BlockSpec(memory_space=pltpu.VMEM)
    dma = pltpu.SemaphoreType.DMA
    return pl.pallas_call(
        functools.partial(kernel, n),
        out_shape=pltpu.VMEM((rows, width), BF16),
        in_specs=[hbm, hbm, hbm, vmem, vmem, vmem],
        out_specs=vmem,
        scratch_shapes=[
            pltpu.VMEM((rows, width), BF16),
            pltpu.VMEM((rows, width), BF16),
            pltpu.VMEM((rows, width), BF16),
            pltpu.VMEM((rows, width), F32),
            pltpu.VMEM((rows, 128), F32),
            pltpu.VMEM((2 + nb, rows, 128), F32),
            pltpu.VMEM((rows, 128), F32),
            pltpu.VMEM((rows, 128), F32),
            pltpu.VMEM((rows, 128), BF16),
            pltpu.VMEM((3, H, DK, DK), BF16),
            pltpu.VMEM((HALF, CW, DK), F32),
            pltpu.VMEM((nb, 8, DK), F32),
            pltpu.VMEM((nb, NC, CW, DK), BF16),
            pltpu.VMEM((nb, NC, CW, DK), BF16),
            pltpu.VMEM((nb, 16, DK), BF16),
            pltpu.VMEM((nb, 16, DK), BF16),
            dma((NC,)), dma((NC,)), dma((NC,)),
            dma((nb, NC)), dma((nb, NC)), dma((nb, NC)), dma((nb,)), dma((nb,)),
        ],
        compiler_params=pltpu.CompilerParams(
            collective_id=0, has_side_effects=True, vmem_limit_bytes=58 * 2**20),
    )(query, key, value, doc_ids.reshape(rows // T, T), gates, gain.reshape(1, width))


def solution(mesh):
    placed = (
        P(("grp", "ctx"), None),
        P(("grp", "ctx"), None),
        P(("grp", "ctx"), None),
        P(("grp", "ctx")),
        P(("grp", "ctx"), None),
        P(),
    )
    return jax.shard_map(
        body, mesh=mesh, in_specs=placed, out_specs=P(("grp", "ctx"), None), check_vma=False
    )
```
